32 devices in a mesh: rows: 8 (over y, x, core), section: 4 (over z).
Axes of the slice: x: 2, y: 2, z: 4, core: 2. Of those that a mesh axis runs over, the one named last changes fastest.
Arguments:
- x_blocks: bfloat16 [96, 4, 2, 128, 128], P('rows', 'section'), may hold values from -2 to 2
- x_cols: int32 [96, 4], P('rows', 'section'), may hold values from -1 to 23, as said below
- c_cols: int32 [96, 12], P('rows', 'section'), may hold values from 0 to 23, as said below
- c_keep: int32 [96, 12], P('rows', 'section'), may hold values 0 or 1
Outputs:
- squared: bfloat16 [96, 12, 2, 128, 128], P('rows', 'section')
The draws below stay inside these ranges and needn't reach their ends.
Inputs may be any that keep to these rules, and one draw needn't show every extreme that they name: `x_cols`: for each block row and panel, the non-empty entries among its 1 slots name distinct columns of the panel; the share of empty slots differs from block row to block row. `c_cols`: for each block row and panel, its 3 entries name distinct columns of the panel.
All inputs are finite; a program needn't handle non-finite values. No bound on the sum of `c_keep` on one device may be relied on, other than what follows from the above.
Results may differ from the reference program's by a relative error of at most 0.001.
Values may be sent and summed in bfloat16 or wider, within the bound.
No kernel may reach another device: no remote copies, remote signals or barrier semaphores. Data moves between devices by JAX's collectives and lax.ppermute only.
A program may use at most 128 MiB of HBM per device.

```python
import jax
import jax.numpy as jnp
from jax import lax

BS = 128
L = 1
LC = 3
NB = 96
PB = 24
NSL = 4
NSC = 12
N_SECTION = 4


def distinct_columns(key, per_panel):
    scores = jax.random.randint(key, (NB, NSL // L, PB), 0, 1 << 16, dtype=jnp.int32) * PB + jnp.arange(PB, dtype=jnp.int32)
    values_unused, picked = lax.top_k(scores, per_panel)
    return picked.reshape(NB, NSL // L * per_panel).astype(jnp.int32)


def stored_columns(key):
    column = distinct_columns(jax.random.fold_in(key, 11), L)
    level = jax.random.randint(jax.random.fold_in(key, 12), (NB, 1), 0, 3, dtype=jnp.int32)
    chance = jax.random.randint(jax.random.fold_in(key, 13), (NB, NSL), 0, 8, dtype=jnp.int32)
    return jnp.where(chance < 2 * level, -1, column).astype(jnp.int32)


def draw_x_cols(key, part):
    return stored_columns(key)


def draw_c_cols(key, part):
    stored = stored_columns(key)
    panels = NSL // L
    slot_ids = jnp.arange(NSL, dtype=jnp.int32)
    present = stored >= 0
    reach_rows = jnp.where(present, (slot_ids // L)[None, :] * PB + stored, 0).astype(jnp.int32)
    far_cols = stored[reach_rows].reshape(NB, NSL, panels, L)
    column_ids = jnp.arange(PB, dtype=jnp.int32)
    reached = (far_cols[:, :, :, :, None] == column_ids) & present[:, :, None, None, None]
    counts = jnp.sum(reached.astype(jnp.int32), axis=(1, 3))
    noise = jax.random.randint(jax.random.fold_in(key, 21), (NB, panels, PB), 0, 4096, dtype=jnp.int32)
    scores = (counts * 4096 + noise) * PB + column_ids
    values_unused, picked = lax.top_k(scores, LC)
    return picked.reshape(NB, panels * LC).astype(jnp.int32)


def set_ends(array, key, low, largest):
    longest = array.shape.index(max(array.shape))
    spots = []
    for shift in (0, 1):
        where = [jax.random.randint(jax.random.fold_in(key, axis), (), 0, length) for axis, length in enumerate(array.shape)]
        where[longest] = (where[longest] + shift) % array.shape[longest]
        spots.append(tuple(where))
    return array.at[spots[0]].set(low).at[spots[1]].set(largest)


def shard_levels(stream_key, extent, cuts, low, largest):
    level = 1.0
    for dim, shards_of in cuts:
        steps = jax.random.uniform(jax.random.fold_in(jax.random.fold_in(stream_key, 6), dim), (shards_of,), jnp.float32, low / len(cuts), largest / len(cuts))
        level = level * jnp.repeat(jnp.exp(steps), extent[dim] // shards_of).reshape((-1,) + (1,) * (len(extent) - 1 - dim))
    return level


def normal_values(own_key, dims, scale, most, shards=(), held_as=jnp.bfloat16):
    loudness = shard_levels(own_key, dims, shards, -0.22, 0.18) if shards else 1.0
    result = jax.random.normal(own_key, dims, jnp.float32) * scale * loudness
    return jnp.minimum(jnp.maximum(result, -most), most).astype(held_as)


def setup_inputs(seed: int = 0) -> dict:
    streams_of = jax.random.split(jax.random.key(seed), 5)
    x_blocks = normal_values(streams_of[0], (NB, NSL, 2, BS, BS), 0.155, 2.0, ((0, 8), (1, 4)))
    x_cols = draw_x_cols(jax.random.fold_in(streams_of[4], 71), 0)
    c_cols = draw_c_cols(jax.random.fold_in(streams_of[4], 71), 0)
    c_keep = set_ends((jax.random.randint(streams_of[3], (NB, NSC), 0, 4) < 3).astype(jnp.int32), jax.random.fold_in(streams_of[3], 1), 0, 1)
    return dict(x_blocks=x_blocks, x_cols=x_cols, c_cols=c_cols, c_keep=c_keep)


def reference(x_blocks, x_cols, c_cols, c_keep):
    slots = jnp.arange(NSL, dtype=jnp.int32)
    panel_of = slots // L

    def one_row(index):
        blocks = x_blocks[index].astype(jnp.float32)
        cols = x_cols[index]
        present = cols >= 0
        rows_needed = jnp.where(present, panel_of * PB + cols, 0).astype(jnp.int32)
        far_blocks = x_blocks[rows_needed].astype(jnp.float32).reshape(NSL, N_SECTION, L, 2, BS, BS)
        far_cols = x_cols[rows_needed].reshape(NSL, N_SECTION, L)
        wanted = c_cols[index].reshape(N_SECTION, LC)
        hits = (far_cols[:, :, None, :] == wanted[None, :, :, None]) & present[:, None, None, None]
        products = jnp.einsum("apxy,aslqyz->aslpqxz", blocks, far_blocks)
        real_part = products[:, :, :, 0, 0] - products[:, :, :, 1, 1]
        imag_part = products[:, :, :, 0, 1] + products[:, :, :, 1, 0]
        complex_terms = jnp.stack([real_part, imag_part], axis=3)
        routed = jnp.einsum("ascl,aslrxz->scrxz", hits.astype(jnp.float32), complex_terms, precision=lax.Precision.HIGHEST)
        return routed.reshape(NSC, 2, BS, BS)

    product = lax.map(one_row, jnp.arange(NB, dtype=jnp.int32))
    kept = c_keep.astype(jnp.float32)[:, :, None, None, None]
    return (product * kept).astype(jnp.bfloat16)
```

```python
import functools

import jax
import jax.numpy as jnp
from jax import lax
from jax.experimental import pallas as pl
from jax.experimental.pallas import tpu as pltpu
from jax.sharding import PartitionSpec as P

FIRST = ((0, 2), (2, 3), (3, 1), (1, 0))
SECOND = ((1, 3), (2, 0), (0, 1), (3, 2))
RELAY = ((2, 3), (1, 0))
MIDDLE = ((2, 1), (1, 2))
THIRD = ((0, 3), (3, 0), (1, 2), (2, 1))


def origin_of(section, *permutations):
    size = max(max(pair) for p in permutations for pair in p) + 1
    tables = [jnp.arange(size, dtype=jnp.int32)]
    for p in permutations:
        source = dict((dst, src) for src, dst in p)
        tables.append(jnp.array([source[d] for d in range(size)], jnp.int32))
    return jnp.stack(tables)[:, section]


def multiply_kernel(
    n_a, n_b, n_panels, per_panel, table, which, *refs
):
    a_bufs, b_bufs = refs[:n_a], refs[n_a : n_a + n_b]
    out, left, right, total, result, load_sem, store_sem = refs[n_a + n_b :]
    rows = out.shape[0]
    slots = n_panels * per_panel

    def fetch(index, carry):
        row, a = index // slots, index % slots

        @pl.when(table[0, row, a] >= 0)
        def _():
            for b in range(n_a):
                @pl.when(which[a // per_panel] == b)
                def _():
                    pltpu.make_async_copy(
                        a_bufs[b].at[row, a % per_panel], left.at[index], load_sem.at[index, 0]
                    ).start()
            for b in range(n_b):
                @pl.when(table[1, row, a] == b)
                def _():
                    pltpu.make_async_copy(
                        b_bufs[b].at[table[2, row, a], 0], right.at[index], load_sem.at[index, 1]
                    ).start()

        return carry

    lax.fori_loop(0, rows * slots, fetch, 0)

    def one_row(row, carry):
        total[...] = jnp.zeros_like(total)

        def one_term(a, inner):
            c = table[0, row, a]

            @pl.when(c >= 0)
            def _():
                index = row * slots + a
                for side, dst in ((0, left), (1, right)):
                    pltpu.make_async_copy(
                        dst.at[index], dst.at[index], load_sem.at[index, side]
                    ).wait()
                b_re, b_im = right[index, 0], right[index, 1]
                lhs = jnp.concatenate([left[index, 0], left[index, 1]], axis=1)
                rhs = jnp.concatenate(
                    [
                        jnp.concatenate([b_re, b_im], axis=1),
                        jnp.concatenate([-b_im, b_re], axis=1),
                    ],
                    axis=0,
                )
                total[c] += jnp.dot(lhs, rhs, preferred_element_type=jnp.float32)

            return inner

        lax.fori_loop(0, slots, one_term, 0)
        bs = result.shape[-1]
        for c in range(result.shape[1]):
            for part in range(2):
                result[row, c, part] = total[c, :, part * bs : (part + 1) * bs].astype(result.dtype)
        pltpu.make_async_copy(result.at[row], out.at[row], store_sem.at[row]).start()
        return carry

    lax.fori_loop(0, rows, one_row, 0)

    def drain(row, carry):
        pltpu.make_async_copy(result.at[row], out.at[row], store_sem.at[row]).wait()
        return carry

    lax.fori_loop(0, rows, drain, 0)


def multiply(table, which, a_bufs, b_bufs, out_shape, per_panel):
    rows, slots = table.shape[1:]
    results, bs = out_shape[1], out_shape[-1]
    n_panels = slots // per_panel
    smem = pl.BlockSpec(memory_space=pltpu.SMEM)
    hbm = pl.BlockSpec(memory_space=pl.ANY)
    return pl.pallas_call(
        functools.partial(
            multiply_kernel, len(a_bufs), len(b_bufs), n_panels, per_panel
        ),
        out_shape=jax.ShapeDtypeStruct(out_shape, jnp.bfloat16),
        in_specs=[smem, smem] + [hbm] * (len(a_bufs) + len(b_bufs)),
        out_specs=hbm,
        scratch_shapes=[
            pltpu.VMEM((rows * slots, 2, bs, bs), jnp.bfloat16),
            pltpu.VMEM((rows * slots, 2, bs, bs), jnp.bfloat16),
            pltpu.VMEM((results, bs, 2 * bs), jnp.float32),
            pltpu.VMEM((rows, results, 2, bs, bs), jnp.bfloat16),
            pltpu.SemaphoreType.DMA((rows * slots, 2)),
            pltpu.SemaphoreType.DMA((rows,)),
        ],
        compiler_params=pltpu.CompilerParams(vmem_limit_bytes=40 * 1024 * 1024),
        cost_estimate=pl.CostEstimate(
            flops=rows * slots * 16 * bs**3, bytes_accessed=16 * rows * slots * bs**2, transcendentals=0
        ),
    )(table, which, *a_bufs, *b_bufs)


def on_device(x_blocks, x_cols, c_cols, c_keep):
    n_rows = lax.axis_size("rows")
    n_section = lax.axis_size("section")
    me_row, me_section = lax.axis_index("rows"), lax.axis_index("section")
    row_count, per_panel, _, bs, _ = x_blocks.shape
    panel_width = row_count * n_rows // n_section
    send = lax.ppermute

    if (n_rows, n_section) == (8, 4):
        swap = lambda x, m: send(x, "rows", [(r, r ^ m) for r in range(n_rows)])
        first = send(x_blocks, "section", FIRST)
        second = send(x_blocks, "section", SECOND)
        along_x, along_y, across = (swap(x_blocks, m) for m in (2, 4, 6))
        middle = send(x_blocks, "section", MIDDLE)
        relayed = send(first, "section", RELAY)
        a_bufs = [x_blocks, first, second, relayed, middle]
        b_bufs = [
            x_blocks, swap(x_blocks, 1), along_x, swap(along_x, 1),
            along_y, swap(along_y, 1), across, swap(across, 1),
        ]
        origin = origin_of(me_section, FIRST, SECOND, THIRD)
        held = jnp.array([0, 1, 2, 3], jnp.int32)
        in_middle = (me_section == 1) | (me_section == 2)
        held = held + ((held == 3) & in_middle)
        which = jnp.sum(
            (origin[None, :] == jnp.arange(4)[:, None]) * held[None, :], axis=1, dtype=jnp.int32
        )
        strips = [x_cols] + [send(x_cols, "section", p) for p in (FIRST, SECOND, THIRD)]
        strip = jnp.stack(strips, axis=1)[:, :, :]
        order = (origin[None, :] == jnp.arange(4)[:, None]).astype(jnp.int32)
        strip = jnp.sum(order[None, :, :, None] * strip[:, None], axis=2).reshape(row_count, -1)
        pieces = x_cols[None]
        for m in (1, 2, 4):
            pieces = jnp.concatenate([pieces, swap(pieces, m)], axis=0)
        mine = lambda group: group ^ me_row
    else:
        shift = lambda x, axis, n, d: send(x, axis, [(p, (p + d) % n) for p in range(n)])
        a_bufs = [x_blocks] + [shift(x_blocks, "section", n_section, d) for d in range(1, n_section)]
        b_bufs = [x_blocks] + [shift(x_blocks, "rows", n_rows, d) for d in range(1, n_rows)]
        which = (me_section - jnp.arange(n_section, dtype=jnp.int32)) % n_section
        strip = lax.all_gather(x_cols, "section", axis=1, tiled=True)
        pieces = jnp.stack([x_cols] + [shift(x_cols, "rows", n_rows, d) for d in range(1, n_rows)])
        mine = lambda group: (me_row - group) % n_rows

    panels = jnp.arange(strip.shape[1], dtype=jnp.int32) // per_panel
    far = jnp.where(strip >= 0, panels[None, :] * panel_width + strip, -1)
    buffer = mine(far // row_count)
    inside = far % row_count
    place = jnp.where(far >= 0, buffer * row_count + inside, -1)
    listed = pieces.reshape(-1)
    hit = place[:, :, None] == jnp.arange(listed.shape[0], dtype=jnp.int32)
    column = jnp.sum(jnp.where(hit, listed + 1, 0), axis=2) - 1
    wanted = jnp.where(c_keep > 0, c_cols, -2)
    match = column[:, :, None] == wanted[:, None, :]
    slot_ids = jnp.arange(wanted.shape[1], dtype=jnp.int32)
    target = jnp.sum(jnp.where(match, slot_ids + 1, 0), axis=2) - 1
    table = jnp.stack([target, buffer, inside]).astype(jnp.int32)
    out_shape = (row_count, c_cols.shape[1], 2, bs, bs)
    return multiply(table, which.astype(jnp.int32), a_bufs, b_bufs, out_shape, per_panel)


def solution(mesh):
    in_specs = (
        P("rows", "section", None, None, None),
        P("rows", "section"),
        P("rows", "section"),
        P("rows", "section"),
    )
    out_specs = P("rows", "section", None, None, None)
    return jax.shard_map(
        on_device, mesh=mesh, in_specs=in_specs, out_specs=out_specs, check_vma=False
    )
```

```python
import functools

import jax
import jax.numpy as jnp
import numpy as np
from jax import lax
from jax.experimental import pallas as pl
from jax.experimental.pallas import tpu as pltpu
from jax.sharding import PartitionSpec as P

RING = (0, 2, 3, 1)
SMEM = pl.BlockSpec(memory_space=pltpu.SMEM)
HBM = pl.BlockSpec(memory_space=pl.ANY)
VMEM = pl.BlockSpec(memory_space=pltpu.VMEM)
LEFT_BUF, LEFT_ROW, RIGHT_BUF, RIGHT_ROW, RESULT, OPENS, CLOSES = range(7)
FIELDS = 7
UNROLL = 4


def plan_kernel(
    sizes, lookup, strip, pieces, c_cols, c_keep, count, terms, empty, column, right_buf, right_row
):
    rows, n_section, n_rows, panel_width, n_early, half = sizes
    left_table = lambda field, a: lookup[field * n_section + a]
    right_table = lambda field, g: lookup[4 * n_section + field * n_rows + g]
    results = c_cols.shape[1]
    count[0] = 0
    count[1] = 0

    def one_row(i, carry):
        in_upper = i >= half
        lefts = [left_table(jnp.where(in_upper, 1, 0), a) for a in range(n_section)]
        left_rows = [i - jnp.where(in_upper, left_table(2, a), 0) for a in range(n_section)]
        for a in range(n_section):
            col = strip[left_table(3, a), i]
            k = jnp.maximum(a * panel_width + col, 0)
            group = k // rows
            inside = k - group * rows
            far = pieces[right_table(3, group), inside]
            column[a] = jnp.where(col >= 0, far, -1)
            upper = inside >= half
            right_buf[a] = right_table(jnp.where(upper, 1, 0), group)
            right_row[a] = inside - jnp.where(upper, right_table(2, group), 0)
        for c in range(results):
            wanted = jnp.where(c_keep[i, c] > 0, c_cols[i, c], -2)
            matches = [(column[a] == wanted).astype(jnp.int32) for a in range(n_section)]
            late = functools.reduce(
                jnp.maximum,
                [m * (lefts[a] >= n_early).astype(jnp.int32) for a, m in enumerate(matches)],
            )
            n_matches = sum(matches)
            empty[i * results + c] = (n_matches == 0).astype(jnp.int32)
            base = count[late]
            seen = jnp.int32(0)
            for a in range(n_section):
                at = base + seen

                @pl.when(matches[a] > 0)
                def _(a=a, at=at, seen=seen):
                    entry = (
                        lefts[a], left_rows[a], right_buf[a], right_row[a], i * results + c,
                        (seen == 0).astype(jnp.int32), (seen == n_matches - 1).astype(jnp.int32),
                    )
                    for f, value in enumerate(entry):
                        terms[late, f, at] = value

                seen = seen + matches[a]
            count[late] = base + n_matches
        return carry

    lax.fori_loop(0, rows, one_row, 0)


def plan(sizes, lookup, strip, pieces, c_cols, c_keep):
    rows, n_section = sizes[:2]
    most = rows * n_section
    return pl.pallas_call(
        functools.partial(plan_kernel, sizes),
        out_shape=(
            jax.ShapeDtypeStruct((2,), jnp.int32),
            jax.ShapeDtypeStruct((2, FIELDS, most), jnp.int32),
            jax.ShapeDtypeStruct((c_cols.size,), jnp.int32),
        ),
        in_specs=[SMEM] * 5,
        out_specs=(SMEM,) * 3,
        scratch_shapes=[pltpu.SMEM((n_section,), jnp.int32)] * 3,
    )(lookup, strip, pieces, c_cols, c_keep)


def multiply_kernel(n_a, n_b, phase, count, terms, empty, *refs):
    a_bufs, b_bufs = refs[:n_a], refs[n_a : n_a + n_b]
    refs = refs[n_a + n_b + (1 if phase else 0) :]
    out, left, right, total, result, zeros, load_sem, store_sem = refs
    results, bs = out.shape[1], out.shape[-1]
    n_terms = count[phase]

    def load(t, side):
        dst = (left, right)[side].at[t]
        return pltpu.make_async_copy(dst, dst, load_sem.at[t, side])

    def store(source, r):
        return pltpu.make_async_copy(source, out.at[r // results, r % results], store_sem.at[r])

    def fetch(t, carry):
        sides = ((a_bufs, LEFT_BUF, LEFT_ROW, left), (b_bufs, RIGHT_BUF, RIGHT_ROW, right))
        for side, (bufs, which, row, dst) in enumerate(sides):
            for b, buf in enumerate(bufs):
                @pl.when(terms[phase, which, t] == b)
                def _():
                    pltpu.make_async_copy(
                        buf.at[pl.ds(pl.multiple_of(terms[phase, row, t] * 2 * bs, 2 * bs), 2 * bs)],
                        dst.at[t],
                        load_sem.at[t, side],
                    ).start()
        return carry

    lax.fori_loop(0, n_terms, fetch, 0)

    def each_empty(step):
        def one(r, carry):
            @pl.when(empty[r] > 0)
            def _():
                step(store(zeros, r))

            return carry

        lax.fori_loop(0, out.shape[0] * results, one, 0)

    if phase == 0:
        zeros[...] = jnp.zeros_like(zeros)
        each_empty(lambda copy: copy.start())

    def some_terms(step, carry):
        ids = [step * UNROLL + u for u in range(UNROLL)]
        for t in ids:
            @pl.when(t < n_terms)
            def _():
                load(t, 0).wait()
                load(t, 1).wait()

        so_far = total[...]
        for t in ids:
            b_re, b_im = right[t, :bs], right[t, bs:]
            lhs = jnp.concatenate([left[t, :bs], left[t, bs:]], axis=1)
            rhs = jnp.concatenate(
                [
                    jnp.concatenate([b_re, b_im], axis=1),
                    jnp.concatenate([-b_im, b_re], axis=1),
                ],
                axis=0,
            )
            product = jnp.dot(lhs, rhs, preferred_element_type=jnp.float32)
            opens = terms[phase, OPENS, t] > 0
            so_far = jnp.where(opens, product, so_far + product)
            for part in range(2):
                result[t, part] = so_far[:, part * bs : (part + 1) * bs].astype(result.dtype)
        total[...] = so_far
        for t in ids:
            @pl.when((t < n_terms) & (terms[phase, CLOSES, t] > 0))
            def _():
                store(result.at[t], terms[phase, RESULT, t]).start()

        return carry

    lax.fori_loop(0, (n_terms + UNROLL - 1) // UNROLL, some_terms, 0)

    def drain(t, carry):
        @pl.when(terms[phase, CLOSES, t] > 0)
        def _():
            store(result.at[t], terms[phase, RESULT, t]).wait()

        return carry

    lax.fori_loop(0, n_terms, drain, 0)
    if phase == 0:
        each_empty(lambda copy: copy.wait())


def multiply(phase, planned, a_bufs, b_bufs, out_shape, so_far=None):
    bs = out_shape[-1]
    n_results = out_shape[0] * out_shape[1]
    most = planned[1].shape[2]
    padded = most + -most % UNROLL
    operands = [*planned, *a_bufs, *b_bufs] + ([] if so_far is None else [so_far])
    return pl.pallas_call(
        functools.partial(multiply_kernel, len(a_bufs), len(b_bufs), phase),
        out_shape=jax.ShapeDtypeStruct(out_shape, jnp.bfloat16),
        in_specs=[SMEM] * 3 + [HBM] * (len(operands) - 3),
        out_specs=HBM,
        scratch_shapes=[
            pltpu.VMEM((padded, 2 * bs, bs), jnp.bfloat16),
            pltpu.VMEM((padded, 2 * bs, bs), jnp.bfloat16),
            pltpu.VMEM((bs, 2 * bs), jnp.float32),
            pltpu.VMEM((padded, 2, bs, bs), jnp.bfloat16),
            pltpu.VMEM((2, bs, bs), jnp.bfloat16),
            pltpu.SemaphoreType.DMA((most, 2)),
            pltpu.SemaphoreType.DMA((n_results,)),
        ],
        input_output_aliases={} if so_far is None else {len(operands) - 1: 0},
        compiler_params=pltpu.CompilerParams(vmem_limit_bytes=48 * 1024 * 1024),
        cost_estimate=pl.CostEstimate(
            flops=most * 16 * bs**3, bytes_accessed=8 * most * bs**2, transcendentals=0
        ),
    )(*operands)


def with_columns(blocks, columns, bs):
    tail = jnp.pad(columns.astype(blocks.dtype)[None], ((0, 15), (0, bs - columns.shape[0])))
    return jnp.concatenate([blocks, tail], axis=0)


def columns_of(sent, rows):
    return sent[-16, :rows].astype(jnp.int32)


def on_device(x_blocks, x_cols, c_cols, c_keep):
    n_rows = lax.axis_size("rows")
    n_section = lax.axis_size("section")
    me_row, me_section = lax.axis_index("rows"), lax.axis_index("section")
    rows, bs = x_blocks.shape[0], x_blocks.shape[-1]
    panel_width = rows * n_rows // n_section
    half = rows // 2
    blocks, columns = x_blocks.reshape(-1, bs), x_cols.reshape(-1)
    everyone = [(r, s) for r in range(n_rows) for s in range(n_section)]

    if (n_rows, n_section) == (8, 4):
        middle = half * 2 * bs
        swap = lambda x, m: lax.ppermute(x, "rows", [(r, r ^ m) for r in range(n_rows)])

        def along(x, way):
            pairs = [(RING[i], RING[(i + way) % 4]) for i in range(4)]
            return lax.ppermute(x, "section", pairs)

        low = [along(with_columns(blocks[:middle], columns, bs), 1)]
        high = [along(with_columns(blocks[middle:], columns, bs), -1)]
        for _ in range(2):
            low.append(along(low[-1], 1))
            high.append(along(high[-1], -1))
        a_bufs = [blocks, *low[:2], *high[:2], low[2], high[2]]
        n_early = 5

        mine = with_columns(blocks, columns, bs)
        b_bufs = [blocks, swap(mine, 1)]
        for m in (2, 4):
            came = swap(mine, m)
            b_bufs += [came, swap(came, 1)]
        across = swap(b_bufs[2][:middle], 4), swap(b_bufs[4][middle:], 2)
        b_bufs += [across[0], swap(across[0], 1), across[1], swap(across[1], 1)]

        strip = [columns] + [columns_of(x, rows) for x in (low[0], high[0], low[1])]
        pieces = [columns] + [columns_of(b_bufs[b], rows) for b in (1, 2, 3, 4, 5, 8, 9)]
        steps = lambda s, a: (RING.index(s) - RING.index(a)) % 4
        tables = [
            [(0, 1, 2, 5)[steps(s, a)] for a in range(4)]
            + [(0, 6, 4, 3)[steps(s, a)] for a in range(4)]
            + [(0, half, half, half)[steps(s, a)] for a in range(4)]
            + [(0, 1, 3, 2)[steps(s, a)] for a in range(4)]
            + [(0, 1, 2, 3, 4, 5, 6, 7)[g ^ r] for g in range(8)]
            + [(0, 1, 2, 3, 4, 5, 8, 9)[g ^ r] for g in range(8)]
            + [(0, 0, 0, 0, 0, 0, half, half)[g ^ r] for g in range(8)]
            + [g ^ r for g in range(8)]
            for r, s in everyone
        ]
    else:

        def shifts(x, axis, n):
            shift = lambda d: lax.ppermute(x, axis, [(p, (p + d) % n) for p in range(n)])
            return [x] + [shift(d) for d in range(1, n)]

        a_bufs, b_bufs = shifts(blocks, "section", n_section), shifts(blocks, "rows", n_rows)
        n_early = len(a_bufs)
        strip, pieces = shifts(columns, "section", n_section), shifts(columns, "rows", n_rows)
        tables = []
        for r, s in everyone:
            panels = [(s - a) % n_section for a in range(n_section)]
            groups = [(r - g) % n_rows for g in range(n_rows)]
            tables.append(panels * 2 + [0] * n_section + panels + groups * 2 + [0] * n_rows + groups)

    lookup = jnp.asarray(np.array(tables, np.int32))[me_row * n_section + me_section]
    sizes = (rows, n_section, n_rows, panel_width, n_early, half)
    planned = plan(sizes, lookup, jnp.stack(strip), jnp.stack(pieces), c_cols, c_keep)
    out_shape = (rows, c_cols.shape[1], *x_blocks.shape[2:])
    out = multiply(0, planned, a_bufs[:n_early], b_bufs, out_shape)
    if n_early < len(a_bufs):
        out = multiply(1, planned, a_bufs, b_bufs, out_shape, out)
    return out


def solution(mesh):
    in_specs = (
        P("rows", "section", None, None, None),
        P("rows", "section"),
        P("rows", "section"),
        P("rows", "section"),
    )
    out_specs = P("rows", "section", None, None, None)
    return jax.shard_map(
        on_device, mesh=mesh, in_specs=in_specs, out_specs=out_specs, check_vma=False
    )
```

```python
import functools

import jax
import jax.numpy as jnp
import numpy as np
from jax import lax
from jax.experimental import pallas as pl
from jax.experimental.pallas import tpu as pltpu
from jax.sharding import PartitionSpec as P

RING = (0, 2, 3, 1)
SMEM = pl.BlockSpec(memory_space=pltpu.SMEM)
HBM = pl.BlockSpec(memory_space=pl.ANY)
LEFT_BUF, LEFT_ROW, RIGHT_BUF, RIGHT_ROW, RESULT, OPENS, CLOSES = range(7)
FIELDS = 7
UNROLL = 4
TAIL = 16
VMEM_BYTES = 60 * 1024 * 1024


def pick(index, low, high, act):
    if high - low == 1:
        act(low)
        return
    middle = (low + high) // 2

    @pl.when(index < middle)
    def _():
        pick(index, low, middle, act)

    @pl.when(index >= middle)
    def _():
        pick(index, middle, high, act)


def make_plan(sizes, lookup, strip, pieces, c_cols, c_keep, results, count, lists, empty):
    rows, n_section, n_rows, panel_width, n_early, half = sizes
    left_table = lambda field, a: lookup(field * n_section + a)
    right_table = lambda field, g: lookup(4 * n_section + field * n_rows + g)
    count[0] = 0
    count[1] = 0

    def one_row(i, carry):
        in_upper = i >= half
        halves = jnp.where(in_upper, 1, 0)
        slots = []
        for a in range(n_section):
            col = strip(left_table(3, a), i)
            k = jnp.maximum(a * panel_width + col, 0)
            group = k // rows
            inside = k - group * rows
            far = jnp.where(col >= 0, pieces(right_table(3, group), inside), -1)
            upper = inside >= half
            slots.append(
                (
                    far, left_table(halves, a), i - jnp.where(in_upper, left_table(2, a), 0),
                    right_table(jnp.where(upper, 1, 0), group),
                    inside - jnp.where(upper, right_table(2, group), 0),
                )
            )
        for c in range(results):
            wanted = jnp.where(c_keep(i, c) > 0, c_cols(i, c), -2)
            matches = [(slot[0] == wanted).astype(jnp.int32) for slot in slots]
            late = functools.reduce(
                jnp.maximum,
                [m * (slot[1] >= n_early).astype(jnp.int32) for m, slot in zip(matches, slots)],
            )
            n_matches = sum(matches)
            empty[i * results + c] = (n_matches == 0).astype(jnp.int32)

            @pl.when(n_matches > 0)
            def _():
                base = count[late]
                seen = jnp.int32(0)
                for m, slot in zip(matches, slots):
                    @pl.when(m > 0)
                    def _():
                        entry = slot[1:] + (
                            i * results + c,
                            (seen == 0).astype(jnp.int32),
                            (seen == n_matches - 1).astype(jnp.int32),
                        )
                        for f, value in enumerate(entry):
                            lists[late, f, base + seen] = value

                    seen = seen + m
                count[late] = base + n_matches

        return carry

    lax.fori_loop(0, rows, one_row, 0)


def multiply(count, terms, empty, a_bufs, b_bufs, out, scratch):
    left, right, total, result, zeros, load_sem, store_sem = scratch
    results, bs = out.shape[1], out.shape[-1]

    def load(t, side):
        dst = (left, right)[side].at[t]
        return pltpu.make_async_copy(dst, dst, load_sem.at[t, side])

    def store(source, r):
        return pltpu.make_async_copy(source, out.at[r // results, r % results], store_sem.at[r])

    def fetch(t, carry):
        sides = ((a_bufs, LEFT_BUF, LEFT_ROW, left), (b_bufs, RIGHT_BUF, RIGHT_ROW, right))
        for side, (bufs, which, row, dst) in enumerate(sides):
            start = pl.multiple_of(terms(row, t) * 2 * bs, 2 * bs)

            def act(b):
                source = bufs[b].at[pl.ds(start, 2 * bs)]
                pltpu.make_async_copy(source, dst.at[t], load_sem.at[t, side]).start()

            pick(terms(which, t), 0, len(bufs), act)
        return carry

    lax.fori_loop(0, count, fetch, 0)

    def each_empty(step):
        def one(r, carry):
            @pl.when(empty[r] > 0)
            def _():
                step(store(zeros, r))

            return carry

        lax.fori_loop(0, out.shape[0] * results, one, 0)

    if empty is not None:
        zeros[...] = jnp.zeros_like(zeros)
        each_empty(lambda copy: copy.start())

    def some_terms(step, carry):
        ids = [step * UNROLL + u for u in range(UNROLL)]
        for t in ids:
            @pl.when(t < count)
            def _():
                load(t, 0).wait()
                load(t, 1).wait()

        so_far = total[...]
        for t in ids:
            b_re, b_im = right[t, :bs], right[t, bs:]
            lhs = jnp.concatenate([left[t, :bs], left[t, bs:]], axis=1)
            rhs = jnp.concatenate(
                [
                    jnp.concatenate([b_re, b_im], axis=1),
                    jnp.concatenate([-b_im, b_re], axis=1),
                ],
                axis=0,
            )
            product = jnp.dot(lhs, rhs, preferred_element_type=jnp.float32)
            so_far = jnp.where(terms(OPENS, t) > 0, product, so_far + product)
            for part in range(2):
                result[t, part] = so_far[:, part * bs : (part + 1) * bs].astype(result.dtype)
        total[...] = so_far
        for t in ids:
            @pl.when((t < count) & (terms(CLOSES, t) > 0))
            def _():
                store(result.at[t], terms(RESULT, t)).start()

        return carry

    lax.fori_loop(0, (count + UNROLL - 1) // UNROLL, some_terms, 0)

    def drain(t, carry):
        @pl.when(terms(CLOSES, t) > 0)
        def _():
            store(result.at[t], terms(RESULT, t)).wait()

        return carry

    lax.fori_loop(0, count, drain, 0)
    if empty is not None:
        each_empty(lambda copy: copy.wait())


def early_kernel(sizes, n_a, n_b, pieces_from, tables, c_cols, c_keep, *refs):
    rows, n_section, n_rows = sizes[:3]
    strips, refs = refs[:n_section], refs[n_section:]
    a_bufs, b_bufs = refs[:n_a], refs[n_a : n_a + n_b]
    (
        out, count_out, late_terms, lists, count, empty, tails, table, numbers, scalars, sem, *scratch
    ) = refs[n_a + n_b :]
    pieces_at = n_section
    wanted_at = pieces_at + n_rows
    keep_at = wanted_at + rows
    lookup_at = keep_at + rows
    me = lax.axis_index("rows") * n_section + lax.axis_index("section")
    copies = [pltpu.make_async_copy(tables.at[me], table, sem.at[0])]
    sources = [*strips, *(b_bufs[b] for b in pieces_from)]
    for n, source in enumerate(sources):
        tail = source.at[pl.ds(source.shape[0] - TAIL, TAIL)]
        copies.append(pltpu.make_async_copy(tail, tails.at[n], sem.at[1 + n]))
    for copy in copies:
        copy.start()
    results = c_cols.shape[1]
    numbers[wanted_at : wanted_at + rows, :results] = c_cols[...]
    numbers[keep_at : keep_at + rows, :results] = c_keep[...]
    for copy in copies:
        copy.wait()
    for n in range(len(sources)):
        numbers[n : n + 1] = tails[n].astype(jnp.float32)[:1].astype(jnp.int32)
    numbers[lookup_at : lookup_at + table.shape[0]] = table[...]
    to_scalars = pltpu.make_async_copy(numbers, scalars, sem.at[0])
    to_scalars.start()
    to_scalars.wait()
    lanes = numbers.shape[1]
    make_plan(
        sizes, lambda n: scalars[lookup_at + n // lanes, n % lanes], lambda n, i: scalars[n, i],
        lambda n, i: scalars[pieces_at + n, i], lambda i, c: scalars[wanted_at + i, c],
        lambda i, c: scalars[keep_at + i, c], results, count, lists, empty,
    )
    count_out[0] = count[1]

    def hand_on(t, carry):
        for f in range(FIELDS):
            late_terms[f, t] = lists[1, f, t]
        return carry

    lax.fori_loop(0, count[1], hand_on, 0)
    multiply(count[0], lambda f, t: lists[0, f, t], empty, a_bufs, b_bufs, out, scratch)


def late_kernel(n_a, n_b, count, terms, *refs):
    a_bufs, b_bufs = refs[:n_a], refs[n_a : n_a + n_b]
    out, *scratch = refs[n_a + n_b + 1 :]
    multiply(count[0], lambda f, t: terms[f, t], None, a_bufs, b_bufs, out, scratch)


def scratch_for(most, n_results, bs):
    padded = most + -most % UNROLL
    return [
        pltpu.VMEM((padded, 2 * bs, bs), jnp.bfloat16),
        pltpu.VMEM((padded, 2 * bs, bs), jnp.bfloat16),
        pltpu.VMEM((bs, 2 * bs), jnp.float32),
        pltpu.VMEM((padded, 2, bs, bs), jnp.bfloat16),
        pltpu.VMEM((2, bs, bs), jnp.bfloat16),
        pltpu.SemaphoreType.DMA((most, 2)),
        pltpu.SemaphoreType.DMA((n_results,)),
    ]


def cost(terms, bs):
    return pl.CostEstimate(
        flops=terms * 16, bytes_accessed=12 * terms, transcendentals=0
    )


def multiply_early(sizes, pieces_from, tables, c_cols, c_keep, strips, a_bufs, b_bufs, out_shape):
    rows, n_section, n_rows = sizes[:3]
    bs, most = out_shape[-1], rows * n_section
    n_results = c_cols.size
    padded = most + -most % UNROLL
    n_numbers = n_section + n_rows + 2 * rows + tables.shape[1]
    vmem = pl.BlockSpec(memory_space=pltpu.VMEM)
    operands = [*strips, *a_bufs, *b_bufs]
    return pl.pallas_call(
        functools.partial(early_kernel, sizes, len(a_bufs), len(b_bufs), pieces_from),
        out_shape=(
            jax.ShapeDtypeStruct(out_shape, jnp.bfloat16),
            jax.ShapeDtypeStruct((1,), jnp.int32),
            jax.ShapeDtypeStruct((FIELDS, padded), jnp.int32),
        ),
        in_specs=[HBM, vmem, vmem] + [HBM] * len(operands),
        out_specs=(HBM, SMEM, SMEM),
        scratch_shapes=[
            pltpu.SMEM((2, FIELDS, padded), jnp.int32),
            pltpu.SMEM((2,), jnp.int32),
            pltpu.SMEM((n_results,), jnp.int32),
            pltpu.VMEM((n_section + n_rows, TAIL, bs), jnp.bfloat16),
            pltpu.VMEM(tables.shape[1:], jnp.int32),
            pltpu.VMEM((n_numbers, bs), jnp.int32),
            pltpu.SMEM((n_numbers, bs), jnp.int32),
            pltpu.SemaphoreType.DMA((1 + n_section + n_rows,)),
            *scratch_for(most, n_results, bs),
        ],
        compiler_params=pltpu.CompilerParams(vmem_limit_bytes=VMEM_BYTES),
        cost_estimate=cost(most, bs),
    )(tables, c_cols, c_keep, *operands)


def multiply_late(count, terms, a_bufs, b_bufs, so_far):
    bs = so_far.shape[-1]
    operands = [count, terms, *a_bufs, *b_bufs, so_far]
    return pl.pallas_call(
        functools.partial(late_kernel, len(a_bufs), len(b_bufs)),
        out_shape=jax.ShapeDtypeStruct(so_far.shape, so_far.dtype),
        in_specs=[SMEM] * 2 + [HBM] * (len(operands) - 2),
        out_specs=HBM,
        scratch_shapes=scratch_for(terms.shape[1], so_far.shape[0] * so_far.shape[1], bs),
        input_output_aliases={len(operands) - 1: 0},
        compiler_params=pltpu.CompilerParams(vmem_limit_bytes=VMEM_BYTES),
        cost_estimate=cost(terms.shape[1] // 4, bs),
    )(*operands)


def with_columns(blocks, *columns):
    bs = blocks.shape[1]
    lines = [jnp.pad(c.astype(blocks.dtype), (0, bs - c.shape[0])) for c in columns]
    tail = jnp.pad(jnp.stack(lines), ((0, TAIL - len(lines)), (0, 0)))
    return jnp.concatenate([blocks, tail], axis=0)


def on_device(x_blocks, x_cols, c_cols, c_keep):
    n_rows = lax.axis_size("rows")
    n_section = lax.axis_size("section")
    rows, bs = x_blocks.shape[0], x_blocks.shape[-1]
    panel_width = rows * n_rows // n_section
    half = rows // 2
    blocks, columns = x_blocks.reshape(-1, bs), x_cols.reshape(-1)
    everyone = [(r, s) for r in range(n_rows) for s in range(n_section)]
    mine = with_columns(blocks, columns)

    if (n_rows, n_section) == (8, 4):
        middle = half * 2 * bs
        swap = lambda x, m: lax.ppermute(x, "rows", [(r, r ^ m) for r in range(n_rows)])

        pairs = [(RING[i], RING[(i + 1) % 4]) for i in range(4)]
        line = jnp.pad(columns.astype(blocks.dtype)[None], ((0, TAIL - 1), (0, bs - rows)))
        line = lax.ppermute(line, "section", [(d, s) for s, d in pairs])
        came = [swap(mine, m) for m in (2, 4, 6)]
        came[0], own, line = lax.optimization_barrier((came[0], mine, line))
        b_bufs = []
        for x in [own, *came]:
            b_bufs += [x, swap(x, 1)]
        pieces_from = tuple(range(8))

        low, high = [with_columns(blocks[:middle], columns)], [blocks[middle:]]
        for _ in range(3):
            low.append(lax.ppermute(low[-1], "section", pairs))
            high.append(lax.ppermute(high[-1], "section", pairs))
        a_bufs = [mine, *low[1:3], *high[1:3], low[3], high[3]]
        n_early = 5
        strips = [mine, *low[1:3], line]

        steps = lambda s, a: (RING.index(s) - RING.index(a)) % 4
        tables = [
            [(0, 1, 2, 5)[steps(s, a)] for a in range(4)]
            + [(0, 3, 4, 6)[steps(s, a)] for a in range(4)]
            + [(0, half, half, half)[steps(s, a)] for a in range(4)]
            + [steps(s, a) for a in range(4)]
            + [g ^ r for g in range(8)] * 2
            + [0] * 8
            + [g ^ r for g in range(8)]
            for r, s in everyone
        ]
    else:

        def shifts(x, axis, n):
            shift = lambda d: lax.ppermute(x, axis, [(p, (p + d) % n) for p in range(n)])
            return [x] + [shift(d) for d in range(1, n)]

        a_bufs, b_bufs = shifts(mine, "section", n_section), shifts(mine, "rows", n_rows)
        strips = a_bufs
        n_early, pieces_from = n_section, tuple(range(n_rows))
        tables = []
        for r, s in everyone:
            panels = [(s - a) % n_section for a in range(n_section)]
            groups = [(r - g) % n_rows for g in range(n_rows)]
            tables.append(panels * 2 + [0] * n_section + panels + groups * 2 + [0] * n_rows + groups)

    tables = np.array(tables, np.int32)
    tables = np.pad(tables, ((0, 0), (0, -tables.shape[1] % (8 * bs)))).reshape(len(everyone), -1, bs)
    sizes = (rows, n_section, n_rows, panel_width, n_early, half)
    out_shape = (rows, c_cols.shape[1], *x_blocks.shape[2:])
    out, count, terms = multiply_early(
        sizes, pieces_from, jnp.asarray(tables), c_cols, c_keep, strips, a_bufs[:n_early], b_bufs, out_shape
    )
    if n_early < len(a_bufs):
        out = multiply_late(count, terms, a_bufs, b_bufs, out)
    return out


def solution(mesh):
    in_specs = (
        P("rows", "section", None, None, None),
        P("rows", "section"),
        P("rows", "section"),
        P("rows", "section"),
    )
    out_specs = P("rows", "section", None, None, None)
    return jax.shard_map(
        on_device, mesh=mesh, in_specs=in_specs, out_specs=out_specs, check_vma=False
    )
```

```python
import functools

import jax
import jax.numpy as jnp
import numpy as np
from jax import lax
from jax.experimental import pallas as pl
from jax.experimental.pallas import tpu as pltpu
from jax.sharding import PartitionSpec as P

RING = (0, 2, 3, 1)
SMEM = pl.BlockSpec(memory_space=pltpu.SMEM)
VMEM = pl.BlockSpec(memory_space=pltpu.VMEM)
HBM = pl.BlockSpec(memory_space=pl.ANY)
UNROLL = 4
TAIL = 16
VMEM_BYTES = 60 * 1024 * 1024
FIELDS = dict(closes=1, opens=1, result=10, left_row=5, left_buf=5, right_row=5, right_buf=4)


def put(**values):
    code, shift = jnp.int32(0), 0
    for field, bits in FIELDS.items():
        if field in values:
            code = code + (values[field] << shift if shift else values[field])
        shift += bits
    return code


def get(code, field):
    shift = 0
    for name, bits in FIELDS.items():
        if name == field:
            return (code >> shift) & ((1 << bits) - 1)
        shift += bits


def pick(index, low, high, act):
    if high - low == 1:
        act(low)
        return
    middle = (low + high) // 2

    @pl.when(index < middle)
    def _():
        pick(index, low, middle, act)

    @pl.when(index >= middle)
    def _():
        pick(index, middle, high, act)


def fetch(t, code, a_bufs, b_bufs, left, right, load_sem):
    size = left.shape[1]
    for side, (bufs, dst, name) in enumerate(((a_bufs, left, "left"), (b_bufs, right, "right"))):
        start = pl.multiple_of(get(code, name + "_row") * size, size)

        def act(b):
            source = bufs[b].at[pl.ds(start, size)]
            pltpu.make_async_copy(source, dst.at[t], load_sem.at[t // UNROLL]).start()

        pick(get(code, name + "_buf"), 0, len(bufs), act)


def store(source, out, r, sem):
    results = out.shape[1]
    return pltpu.make_async_copy(source, out.at[r // results, r % results], sem)


def multiply(count, codes, out, left, right, total, result, load_sem, store_sem):
    bs = out.shape[-1]

    def some_terms(step, carry):
        ids = [step * UNROLL + u for u in range(UNROLL)]
        for t in ids:
            @pl.when(t < count)
            def _():
                for dst in (left, right):
                    pltpu.make_async_copy(dst.at[t], dst.at[t], load_sem.at[step]).wait()

        so_far = total[...]
        for t in ids:
            b_re, b_im = right[t, :bs], right[t, bs:]
            lhs = jnp.concatenate([left[t, :bs], left[t, bs:]], axis=1)
            rhs = jnp.concatenate(
                [
                    jnp.concatenate([b_re, b_im], axis=1),
                    jnp.concatenate([-b_im, b_re], axis=1),
                ],
                axis=0,
            )
            product = jnp.dot(lhs, rhs, preferred_element_type=jnp.float32)
            so_far = jnp.where(get(codes(t), "opens") > 0, product, so_far + product)
            for part in range(2):
                result[t, part] = so_far[:, part * bs : (part + 1) * bs].astype(result.dtype)
        total[...] = so_far
        for t in ids:
            code = codes(t)

            @pl.when((t < count) & (get(code, "closes") > 0))
            def _():
                store(result.at[t], out, get(code, "result"), store_sem).start()

        return carry

    lax.fori_loop(0, (count + UNROLL - 1) // UNROLL, some_terms, 0)

    def drain(t, carry):
        code = codes(t)

        @pl.when(get(code, "closes") > 0)
        def _():
            store(result.at[t], out, get(code, "result"), store_sem).wait()

        return carry

    lax.fori_loop(0, count, drain, 0)


def early_kernel(sizes, n_a, n_b, tables, c_cols, c_keep, *refs):
    rows, n_section, n_rows, panel_width, n_early, half = sizes
    strips, refs = refs[:n_section], refs[n_section:]
    a_bufs, b_bufs = refs[:n_a], refs[n_a : n_a + n_b]
    (
        out, late_codes, codes, empty, tails, table, numbers, scalars, zeros, sem, *scratch
    ) = refs[n_a + n_b :]
    left, right, _, _, load_sem, store_sem = scratch
    pieces_at = n_section
    wanted_at = pieces_at + n_rows
    keep_at = wanted_at + rows
    lookup_at = keep_at + rows
    results = c_cols.shape[1]
    me = lax.axis_index("rows") * n_section + lax.axis_index("section")
    copies = [pltpu.make_async_copy(tables.at[me], table, sem.at[0])]
    sources = [*strips, *b_bufs]
    for n, source in enumerate(sources):
        tail = source.at[pl.ds(source.shape[0] - TAIL, TAIL)]
        copies.append(pltpu.make_async_copy(tail, tails.at[n], sem.at[1]))
    for copy in copies:
        copy.start()
    zeros[...] = jnp.zeros_like(zeros)
    numbers[wanted_at : wanted_at + rows, :results] = jnp.where(c_keep[...] > 0, c_cols[...], -2)
    for copy in copies:
        copy.wait()
    for n in range(len(sources)):
        numbers[n : n + 1] = tails[n].astype(jnp.float32)[:1].astype(jnp.int32)
    numbers[lookup_at : lookup_at + table.shape[0]] = table[...]
    to_scalars = pltpu.make_async_copy(numbers, scalars, sem.at[0])
    to_scalars.start()
    to_scalars.wait()
    lanes = numbers.shape[1]

    def lookup(n):
        return scalars[lookup_at + n // lanes, n % lanes]

    def one_row(i, counts):
        in_upper = i >= half
        columns, lates, parts = [], [], []
        for a in range(n_section):
            col = scalars[lookup(3 * n_section + a), i]
            k = jnp.maximum(a * panel_width + col, 0)
            group = k // rows
            inside = k - group * rows
            piece = scalars[lookup_at + (4 * n_section) // lanes, (4 * n_section) % lanes + group]
            columns.append(jnp.where(col >= 0, scalars[pieces_at + piece, inside], -1))
            buf = jnp.where(in_upper, lookup(n_section + a), lookup(a))
            lates.append((buf >= n_early).astype(jnp.int32))
            row = i - jnp.where(in_upper, lookup(2 * n_section + a), 0)
            parts.append(put(left_buf=buf, left_row=row, right_buf=piece, right_row=inside))
        n_now, n_late = counts
        for c in range(results):
            r = i * results + c
            wanted = scalars[wanted_at + i, c]
            matches = [(column == wanted).astype(jnp.int32) for column in columns]
            n_matches = sum(matches)
            late = functools.reduce(jnp.maximum, [m * l for m, l in zip(matches, lates)])
            empty[r] = n_matches

            @pl.when(n_matches == 0)
            def _():
                store(zeros, out, r, store_sem).start()

            @pl.when(n_matches > 0)
            def _():
                seen = jnp.int32(0)
                for m, part in zip(matches, parts):
                    @pl.when(m > 0)
                    def _():
                        opens = (seen == 0).astype(jnp.int32)
                        closes = (seen == n_matches - 1).astype(jnp.int32)
                        code = part + put(result=r, opens=opens, closes=closes)

                        @pl.when(late > 0)
                        def _():
                            late_codes[1 + n_late + seen] = code

                        @pl.when(late == 0)
                        def _():
                            codes[n_now + seen] = code
                            fetch(n_now + seen, code, a_bufs, b_bufs, left, right, load_sem)

                    seen = seen + m

            n_late = n_late + n_matches * late
            n_now = n_now + n_matches * (1 - late)
        return n_now, n_late

    n_now, n_late = lax.fori_loop(0, rows, one_row, (jnp.int32(0), jnp.int32(0)))
    late_codes[0] = n_late
    multiply(n_now, lambda t: codes[t], out, *scratch)

    def drain(r, carry):
        @pl.when(empty[r] == 0)
        def _():
            store(zeros, out, r, store_sem).wait()

        return carry

    lax.fori_loop(0, rows * results, drain, 0)


def late_kernel(n_a, n_b, codes, *refs):
    a_bufs, b_bufs = refs[:n_a], refs[n_a : n_a + n_b]
    out, *scratch = refs[n_a + n_b + 1 :]
    left, right, _, _, load_sem, _ = scratch

    def one(t, carry):
        fetch(t, codes[1 + t], a_bufs, b_bufs, left, right, load_sem)
        return carry

    lax.fori_loop(0, codes[0], one, 0)
    multiply(codes[0], lambda t: codes[1 + t], out, *scratch)


def scratch_for(most, bs):
    return [
        pltpu.VMEM((most, 2 * bs, bs), jnp.bfloat16),
        pltpu.VMEM((most, 2 * bs, bs), jnp.bfloat16),
        pltpu.VMEM((bs, 2 * bs), jnp.float32),
        pltpu.VMEM((most, 2, bs, bs), jnp.bfloat16),
        pltpu.SemaphoreType.DMA((most // UNROLL,)),
        pltpu.SemaphoreType.DMA,
    ]


def multiply_early(sizes, tables, c_cols, c_keep, strips, a_bufs, b_bufs, out_shape):
    rows, n_section, n_rows = sizes[:3]
    operands = [*strips, *a_bufs, *b_bufs]
    bs, n_results = out_shape[-1], c_cols.size
    most = rows * n_section + -(rows * n_section) % UNROLL
    n_tails = n_section + n_rows
    n_numbers = n_tails + 2 * rows + tables.shape[1]
    return pl.pallas_call(
        functools.partial(early_kernel, sizes, len(a_bufs), len(b_bufs)),
        out_shape=(
            jax.ShapeDtypeStruct(out_shape, jnp.bfloat16),
            jax.ShapeDtypeStruct((1 + most,), jnp.int32),
        ),
        in_specs=[HBM, VMEM, VMEM] + [HBM] * len(operands),
        out_specs=(HBM, SMEM),
        scratch_shapes=[
            pltpu.SMEM((most,), jnp.int32),
            pltpu.SMEM((n_results,), jnp.int32),
            pltpu.VMEM((n_tails, TAIL, bs), jnp.bfloat16),
            pltpu.VMEM(tables.shape[1:], jnp.int32),
            pltpu.VMEM((n_numbers, bs), jnp.int32),
            pltpu.SMEM((n_numbers, bs), jnp.int32),
            pltpu.VMEM((2, bs, bs), jnp.bfloat16),
            pltpu.SemaphoreType.DMA((2,)),
            *scratch_for(most, bs),
        ],
        compiler_params=pltpu.CompilerParams(vmem_limit_bytes=VMEM_BYTES),
        cost_estimate=pl.CostEstimate(flops=1000, bytes_accessed=1000, transcendentals=0),
    )(tables, c_cols, c_keep, *operands)


def multiply_late(codes, a_bufs, b_bufs, so_far):
    operands = [codes, *a_bufs, *b_bufs, so_far]
    return pl.pallas_call(
        functools.partial(late_kernel, len(a_bufs), len(b_bufs)),
        out_shape=jax.ShapeDtypeStruct(so_far.shape, so_far.dtype),
        in_specs=[SMEM] + [HBM] * (len(operands) - 1),
        out_specs=HBM,
        scratch_shapes=scratch_for(codes.shape[0] - 1, so_far.shape[-1]),
        input_output_aliases={len(operands) - 1: 0},
        compiler_params=pltpu.CompilerParams(vmem_limit_bytes=VMEM_BYTES),
    )(*operands)


def on_device(x_blocks, x_cols, c_cols, c_keep):
    n_rows = lax.axis_size("rows")
    n_section = lax.axis_size("section")
    rows, bs = x_blocks.shape[0], x_blocks.shape[-1]
    panel_width = rows * n_rows // n_section
    half = rows // 2
    blocks, columns = x_blocks.reshape(-1, bs), x_cols.reshape(-1)
    everyone = [(r, s) for r in range(n_rows) for s in range(n_section)]
    tail = jnp.pad(columns.astype(blocks.dtype)[None], ((0, TAIL - 1), (0, bs - rows)))
    mine = jnp.concatenate([blocks, tail])

    if (n_rows, n_section) == (8, 4):
        swap = lambda x, m: lax.ppermute(x, "rows", [(r, r ^ m) for r in range(n_rows)])

        pairs = [(RING[i], RING[(i + 1) % 4]) for i in range(4)]
        step = lambda x: lax.ppermute(x, "section", pairs)
        half = 3
        middle = half * 2 * bs
        small, big = [jnp.concatenate([blocks[:middle], tail])], [blocks[middle:]]
        small.append(step(small[0]))
        big.append(step(big[0]))
        for_across = own = mine
        for_across, small[1] = lax.optimization_barrier((mine, small[1]))
        for _ in range(2):
            small.append(step(small[-1]))
            big.append(step(big[-1]))

        came = [swap(mine, 2), swap(mine, 4), swap(for_across, 6)]
        b_bufs = []
        for x in [own, *came]:
            b_bufs += [x, swap(x, 1)]
        a_bufs = [mine, *small[1:], *big[1:]]
        n_early = 6
        strips = [mine, *small[1:]]

        steps = lambda s, a: (RING.index(s) - RING.index(a)) % 4
        tables = [
            [steps(s, a) for a in range(4)]
            + [(0, 4, 5, 6)[steps(s, a)] for a in range(4)]
            + [(0, half, half, half)[steps(s, a)] for a in range(4)]
            + [steps(s, a) for a in range(4)]
            + [g ^ r for g in range(8)]
            for r, s in everyone
        ]
    else:

        def shifts(x, axis, n):
            shift = lambda d: lax.ppermute(x, axis, [(p, (p + d) % n) for p in range(n)])
            return [x] + [shift(d) for d in range(1, n)]

        a_bufs, b_bufs = shifts(mine, "section", n_section), shifts(mine, "rows", n_rows)
        n_early, strips = n_section, a_bufs
        tables = []
        for r, s in everyone:
            panels = [(s - a) % n_section for a in range(n_section)]
            groups = [(r - g) % n_rows for g in range(n_rows)]
            tables.append(panels * 2 + [0] * n_section + panels + groups)

    tables = np.array(tables, np.int32)
    tables = np.pad(tables, ((0, 0), (0, -tables.shape[1] % (8 * bs)))).reshape(len(everyone), -1, bs)
    sizes = (rows, n_section, n_rows, panel_width, n_early, half)
    out_shape = (rows, c_cols.shape[1], *x_blocks.shape[2:])
    out, codes = multiply_early(
        sizes, jnp.asarray(tables), c_cols, c_keep, strips, a_bufs[:n_early], b_bufs, out_shape
    )
    if n_early < len(a_bufs):
        out = multiply_late(codes, a_bufs, b_bufs, out)
    return out


def solution(mesh):
    in_specs = (
        P("rows", "section", None, None, None),
        P("rows", "section"),
        P("rows", "section"),
        P("rows", "section"),
    )
    out_specs = P("rows", "section", None, None, None)
    return jax.shard_map(
        on_device, mesh=mesh, in_specs=in_specs, out_specs=out_specs, check_vma=False
    )
```

```python
import functools

import jax
import jax.numpy as jnp
import numpy as np
from jax import lax
from jax.experimental import pallas as pl
from jax.experimental.pallas import tpu as pltpu
from jax.sharding import PartitionSpec as P

RING = (0, 2, 3, 1)
SMEM = pl.BlockSpec(memory_space=pltpu.SMEM)
VMEM = pl.BlockSpec(memory_space=pltpu.VMEM)
HBM = pl.BlockSpec(memory_space=pl.ANY)
UNROLL = 4
TAIL = 16
VMEM_BYTES = 60 * 1024 * 1024
FIELDS = dict(closes=1, opens=1, result=10, left_row=5, left_buf=5, right_row=5, right_buf=4)


def put(**values):
    code, shift = jnp.int32(0), 0
    for field, bits in FIELDS.items():
        if field in values:
            code = code + (values[field] << shift if shift else values[field])
        shift += bits
    return code


def get(code, field):
    shift = 0
    for name, bits in FIELDS.items():
        if name == field:
            return (code >> shift) & ((1 << bits) - 1)
        shift += bits


def pick(index, low, high, act):
    if high - low == 1:
        act(low)
        return
    middle = (low + high) // 2

    @pl.when(index < middle)
    def _():
        pick(index, low, middle, act)

    @pl.when(index >= middle)
    def _():
        pick(index, middle, high, act)


def fetch(t, code, a_bufs, b_bufs, left, right, load_sem):
    size = left.shape[1]
    for side, (bufs, dst, name) in enumerate(((a_bufs, left, "left"), (b_bufs, right, "right"))):
        start = pl.multiple_of(get(code, name + "_row") * size, size)

        def act(b):
            source = bufs[b].at[pl.ds(start, size)]
            pltpu.make_async_copy(source, dst.at[t], load_sem.at[t // UNROLL]).start()

        pick(get(code, name + "_buf"), 0, len(bufs), act)


def store(source, out, r, sem):
    results = out.shape[1]
    return pltpu.make_async_copy(source, out.at[r // results, r % results], sem)


def multiply(count, codes, out, left, right, total, result, load_sem, store_sem):
    bs = out.shape[-1]

    def some_terms(step, carry):
        ids = [step * UNROLL + u for u in range(UNROLL)]
        for t in ids:
            @pl.when(t < count)
            def _():
                for dst in (left, right):
                    pltpu.make_async_copy(dst.at[t], dst.at[t], load_sem.at[step]).wait()

        so_far = total[...]
        for t in ids:
            b_re, b_im = right[t, :bs], right[t, bs:]
            lhs = jnp.concatenate([left[t, :bs], left[t, bs:]], axis=1)
            rhs = jnp.concatenate(
                [
                    jnp.concatenate([b_re, b_im], axis=1),
                    jnp.concatenate([-b_im, b_re], axis=1),
                ],
                axis=0,
            )
            product = jnp.dot(lhs, rhs, preferred_element_type=jnp.float32)
            so_far = jnp.where(get(codes(t), "opens") > 0, product, so_far + product)
            for part in range(2):
                result[t, part] = so_far[:, part * bs : (part + 1) * bs].astype(result.dtype)
        total[...] = so_far
        for t in ids:
            code = codes(t)

            @pl.when((t < count) & (get(code, "closes") > 0))
            def _():
                store(result.at[t], out, get(code, "result"), store_sem).start()

        return carry

    lax.fori_loop(0, (count + UNROLL - 1) // UNROLL, some_terms, 0)

    def drain(t, carry):
        code = codes(t)

        @pl.when(get(code, "closes") > 0)
        def _():
            store(result.at[t], out, get(code, "result"), store_sem).wait()

        return carry

    lax.fori_loop(0, count, drain, 0)


def early_kernel(sizes, n_a, n_b, pieces_from, tables, c_cols, c_keep, *refs):
    rows, n_section, n_rows, panel_width, n_early, half = sizes
    strips, refs = refs[:n_section], refs[n_section:]
    a_bufs, b_bufs = refs[:n_a], refs[n_a : n_a + n_b]
    (
        out, late_codes, codes, empty, tails, table, numbers, scalars, zeros, sem, *scratch
    ) = refs[n_a + n_b :]
    left, right, _, _, load_sem, store_sem = scratch
    pieces_at = n_section
    wanted_at = pieces_at + n_rows
    lookup_at = wanted_at + rows
    results = c_cols.shape[1]
    me = lax.axis_index("rows") * n_section + lax.axis_index("section")
    copies = [pltpu.make_async_copy(tables.at[me], table, sem.at[0])]
    sources = [*strips, *(b_bufs[b] for b in pieces_from)]
    for n, source in enumerate(sources):
        tail = source.at[pl.ds(source.shape[0] - TAIL, TAIL)]
        copies.append(pltpu.make_async_copy(tail, tails.at[n], sem.at[1]))
    for copy in copies:
        copy.start()
    zeros[...] = jnp.zeros_like(zeros)
    numbers[wanted_at : wanted_at + rows, :results] = jnp.where(c_keep[...] > 0, c_cols[...], -2)
    for copy in copies:
        copy.wait()
    for n in range(len(sources)):
        numbers[n : n + 1] = tails[n].astype(jnp.float32)[:1].astype(jnp.int32)
    numbers[lookup_at : lookup_at + 1] = table[:1]
    to_scalars = pltpu.make_async_copy(numbers, scalars, sem.at[0])
    to_scalars.start()
    to_scalars.wait()

    def lookup(n):
        return scalars[lookup_at, n]

    reciprocal = -(-(1 << 16) // rows)
    ks = np.arange(n_rows * rows)
    assert (ks * reciprocal >> 16 == ks // rows).all()
    low_bufs, high_bufs, cuts, strip_of = (
        [lookup(f * n_section + a) for a in range(n_section)] for f in range(4)
    )

    def one_row(i, counts):
        in_upper = i >= half
        columns, lates, parts = [], [], []
        for a in range(n_section):
            col = scalars[strip_of[a], i]
            k = jnp.maximum(a * panel_width + col, 0)
            group = (k * reciprocal) >> 16
            inside = k - group * rows
            piece = lookup(4 * n_section + 3 * n_rows + group)
            columns.append(jnp.where(col >= 0, scalars[pieces_at + piece, inside], -1))
            upper = inside >= rows // 2
            source = lookup(4 * n_section + jnp.where(upper, n_rows, 0) + group)
            inside = inside - jnp.where(upper, lookup(4 * n_section + 2 * n_rows + group), 0)
            buf = jnp.where(in_upper, high_bufs[a], low_bufs[a])
            lates.append((buf >= n_early).astype(jnp.int32))
            row = i - jnp.where(in_upper, cuts[a], 0)
            parts.append(put(left_buf=buf, left_row=row, right_buf=source, right_row=inside))
        n_now, n_late = counts
        for c in range(results):
            r = i * results + c
            wanted = scalars[wanted_at + i, c]
            matches = [(column == wanted).astype(jnp.int32) for column in columns]
            n_matches = sum(matches)
            late = functools.reduce(jnp.maximum, [m * l for m, l in zip(matches, lates)])
            empty[r] = n_matches

            @pl.when(n_matches == 0)
            def _():
                store(zeros, out, r, store_sem).start()

            @pl.when(n_matches > 0)
            def _():
                seen = jnp.int32(0)
                for m, part in zip(matches, parts):
                    @pl.when(m > 0)
                    def _():
                        opens = (seen == 0).astype(jnp.int32)
                        closes = (seen == n_matches - 1).astype(jnp.int32)
                        code = part + put(result=r, opens=opens, closes=closes)

                        @pl.when(late > 0)
                        def _():
                            late_codes[1 + n_late + seen] = code

                        @pl.when(late == 0)
                        def _():
                            codes[n_now + seen] = code
                            fetch(n_now + seen, code, a_bufs, b_bufs, left, right, load_sem)

                    seen = seen + m

            n_late = n_late + n_matches * late
            n_now = n_now + n_matches * (1 - late)
        return n_now, n_late

    n_now, n_late = lax.fori_loop(0, rows, one_row, (jnp.int32(0), jnp.int32(0)))
    late_codes[0] = n_late
    multiply(n_now, lambda t: codes[t], out, *scratch)

    def drain(r, carry):
        @pl.when(empty[r] == 0)
        def _():
            store(zeros, out, r, store_sem).wait()

        return carry

    lax.fori_loop(0, rows * results, drain, 0)


def late_kernel(n_a, n_b, codes, *refs):
    a_bufs, b_bufs = refs[:n_a], refs[n_a : n_a + n_b]
    out, *scratch = refs[n_a + n_b + 1 :]
    left, right, _, _, load_sem, _ = scratch

    def one(t, carry):
        fetch(t, codes[1 + t], a_bufs, b_bufs, left, right, load_sem)
        return carry

    lax.fori_loop(0, codes[0], one, 0)
    multiply(codes[0], lambda t: codes[1 + t], out, *scratch)


def scratch_for(most, bs):
    return [
        pltpu.VMEM((most, 2 * bs, bs), jnp.bfloat16),
        pltpu.VMEM((most, 2 * bs, bs), jnp.bfloat16),
        pltpu.VMEM((bs, 2 * bs), jnp.float32),
        pltpu.VMEM((most, 2, bs, bs), jnp.bfloat16),
        pltpu.SemaphoreType.DMA((most // UNROLL,)),
        pltpu.SemaphoreType.DMA,
    ]


def multiply_early(sizes, pieces_from, tables, c_cols, c_keep, strips, a_bufs, b_bufs, out_shape):
    rows, n_section, n_rows = sizes[:3]
    operands = [*strips, *a_bufs, *b_bufs]
    bs, n_results = out_shape[-1], c_cols.size
    most = rows * n_section + -(rows * n_section) % UNROLL
    n_tails = n_section + n_rows
    n_numbers = n_tails + rows + 1
    return pl.pallas_call(
        functools.partial(early_kernel, sizes, len(a_bufs), len(b_bufs), pieces_from),
        out_shape=(
            jax.ShapeDtypeStruct(out_shape, jnp.bfloat16),
            jax.ShapeDtypeStruct((1 + most,), jnp.int32),
        ),
        in_specs=[HBM, VMEM, VMEM] + [HBM] * len(operands),
        out_specs=(HBM, SMEM),
        scratch_shapes=[
            pltpu.SMEM((most,), jnp.int32),
            pltpu.SMEM((n_results,), jnp.int32),
            pltpu.VMEM((n_tails, TAIL, bs), jnp.bfloat16),
            pltpu.VMEM(tables.shape[1:], jnp.int32),
            pltpu.VMEM((n_numbers, bs), jnp.int32),
            pltpu.SMEM((n_numbers, bs), jnp.int32),
            pltpu.VMEM((2, bs, bs), jnp.bfloat16),
            pltpu.SemaphoreType.DMA((2,)),
            *scratch_for(most, bs),
        ],
        compiler_params=pltpu.CompilerParams(vmem_limit_bytes=VMEM_BYTES),
        cost_estimate=pl.CostEstimate(flops=1000, bytes_accessed=1000, transcendentals=0),
    )(tables, c_cols, c_keep, *operands)


def multiply_late(codes, a_bufs, b_bufs, so_far):
    operands = [codes, *a_bufs, *b_bufs, so_far]
    return pl.pallas_call(
        functools.partial(late_kernel, len(a_bufs), len(b_bufs)),
        out_shape=jax.ShapeDtypeStruct(so_far.shape, so_far.dtype),
        in_specs=[SMEM] + [HBM] * (len(operands) - 1),
        out_specs=HBM,
        scratch_shapes=scratch_for(codes.shape[0] - 1, so_far.shape[-1]),
        input_output_aliases={len(operands) - 1: 0},
        compiler_params=pltpu.CompilerParams(vmem_limit_bytes=VMEM_BYTES),
    )(*operands)


def on_device(x_blocks, x_cols, c_cols, c_keep):
    n_rows = lax.axis_size("rows")
    n_section = lax.axis_size("section")
    rows, bs = x_blocks.shape[0], x_blocks.shape[-1]
    panel_width = rows * n_rows // n_section
    half = rows // 2
    blocks, columns = x_blocks.reshape(-1, bs), x_cols.reshape(-1)
    everyone = [(r, s) for r in range(n_rows) for s in range(n_section)]
    tail = jnp.pad(columns.astype(blocks.dtype)[None], ((0, TAIL - 1), (0, bs - rows)))
    mine = jnp.concatenate([blocks, tail])

    if (n_rows, n_section) == (8, 4):
        swap = lambda x, m: lax.ppermute(x, "rows", [(r, r ^ m) for r in range(n_rows)])

        pairs = [(RING[i], RING[(i + 1) % 4]) for i in range(4)]
        step = lambda x: lax.ppermute(x, "section", pairs)
        half = 4
        middle = half * 2 * bs
        small, big = [jnp.concatenate([blocks[:middle], tail])], [blocks[middle:]]
        small.append(step(small[0]))
        big.append(step(big[0]))

        for_d, small[1] = lax.optimization_barrier((mine, small[1]))
        came = [swap(mine, 2), swap(mine, 4), swap(for_d, 6)]
        beside = swap(mine, 1)
        small.append(step(small[1]))
        big.append(step(big[1]))
        small.append(step(small[2]))
        past = [swap(came[0], 1), swap(came[1], 1)]
        big[2], beside = lax.optimization_barrier((big[2], beside))
        big.append(step(big[2]))

        cut = rows // 2 * 2 * bs
        lower, upper = came[2][:cut], came[2][cut:]
        lower, small[3] = lax.optimization_barrier((lower, small[3]))
        b_bufs = [mine, beside, *came, *past, swap(lower, 1), swap(upper, 1)]
        a_bufs = [mine, *small[1:], *big[1:]]
        n_early = 6
        strips = [mine, *small[1:]]

        pieces_from = (0, 1, 2, 5, 3, 6, 4, 8)
        steps = lambda s, a: (RING.index(s) - RING.index(a)) % 4
        tables = [
            [steps(s, a) for a in range(4)]
            + [(0, 4, 5, 6)[steps(s, a)] for a in range(4)]
            + [(0, half, half, half)[steps(s, a)] for a in range(4)]
            + [steps(s, a) for a in range(4)]
            + [(0, 1, 2, 5, 3, 6, 4, 7)[g ^ r] for g in range(8)]
            + [(0, 1, 2, 5, 3, 6, 4, 8)[g ^ r] for g in range(8)]
            + [(0, 0, 0, 0, 0, 0, 0, rows // 2)[g ^ r] for g in range(8)]
            + [g ^ r for g in range(8)]
            for r, s in everyone
        ]
    else:

        def shifts(x, axis, n):
            shift = lambda d: lax.ppermute(x, axis, [(p, (p + d) % n) for p in range(n)])
            return [x] + [shift(d) for d in range(1, n)]

        a_bufs, b_bufs = shifts(mine, "section", n_section), shifts(mine, "rows", n_rows)
        n_early, strips = n_section, a_bufs
        pieces_from = tuple(range(n_rows))
        tables = []
        for r, s in everyone:
            panels = [(s - a) % n_section for a in range(n_section)]
            groups = [(r - g) % n_rows for g in range(n_rows)]
            tables.append(panels * 2 + [0] * n_section + panels + groups * 2 + [0] * n_rows + groups)

    tables = np.array(tables, np.int32)
    assert tables.shape[1] <= bs
    tables = np.pad(tables, ((0, 0), (0, 8 * bs - tables.shape[1]))).reshape(len(everyone), 8, bs)
    sizes = (rows, n_section, n_rows, panel_width, n_early, half)
    out_shape = (rows, c_cols.shape[1], *x_blocks.shape[2:])
    out, codes = multiply_early(
        sizes, pieces_from, jnp.asarray(tables), c_cols, c_keep, strips, a_bufs[:n_early], b_bufs, out_shape
    )
    if n_early < len(a_bufs):
        out = multiply_late(codes, a_bufs, b_bufs, out)
    return out


def solution(mesh):
    in_specs = (
        P("rows", "section", None, None, None),
        P("rows", "section"),
        P("rows", "section"),
        P("rows", "section"),
    )
    out_specs = P("rows", "section", None, None, None)
    return jax.shard_map(
        on_device, mesh=mesh, in_specs=in_specs, out_specs=out_specs, check_vma=False
    )
```

```python
import functools

import jax
import jax.numpy as jnp
import numpy as np
from jax import lax
from jax.experimental import pallas as pl
from jax.experimental.pallas import tpu as pltpu
from jax.sharding import PartitionSpec as P

RING = (0, 2, 3, 1)
SMEM = pl.BlockSpec(memory_space=pltpu.SMEM)
VMEM = pl.BlockSpec(memory_space=pltpu.VMEM)
HBM = pl.BlockSpec(memory_space=pl.ANY)
UNROLL = 8
TAIL = 16
VMEM_BYTES = 60 * 1024 * 1024
FIELDS = dict(closes=1, opens=1, result=10, left_row=5, left_buf=5, right_row=5, right_buf=4)


def put(**values):
    code, shift = jnp.int32(0), 0
    for field, bits in FIELDS.items():
        if field in values:
            code = code + (values[field] << shift if shift else values[field])
        shift += bits
    return code


def get(code, field):
    shift = 0
    for name, bits in FIELDS.items():
        if name == field:
            return (code >> shift) & ((1 << bits) - 1)
        shift += bits


def pick(index, low, high, act):
    if high - low == 1:
        act(low)
        return
    middle = (low + high) // 2

    @pl.when(index < middle)
    def _():
        pick(index, low, middle, act)

    @pl.when(index >= middle)
    def _():
        pick(index, middle, high, act)


def fetch(t, code, a_bufs, b_bufs, left, right, load_sem):
    size = left.shape[1]
    for side, (bufs, dst, name) in enumerate(((a_bufs, left, "left"), (b_bufs, right, "right"))):
        start = pl.multiple_of(get(code, name + "_row") * size, size)

        def act(b):
            source = bufs[b].at[pl.ds(start, size)]
            pltpu.make_async_copy(source, dst.at[t], load_sem.at[t // UNROLL]).start()

        pick(get(code, name + "_buf"), 0, len(bufs), act)


def store(source, out, r, sem):
    results = out.shape[1]
    return pltpu.make_async_copy(source, out.at[r // results, r % results], sem)


def multiply(count, codes, out, left, right, total, result, load_sem, store_sem):
    bs = out.shape[-1]

    def some_terms(step, carry):
        ids = [step * UNROLL + u for u in range(UNROLL)]
        for t in ids:
            @pl.when(t < count)
            def _():
                for dst in (left, right):
                    pltpu.make_async_copy(dst.at[t], dst.at[t], load_sem.at[step]).wait()

        so_far = total[...]
        for t in ids:
            b_re, b_im = right[t, :bs], right[t, bs:]
            lhs = jnp.concatenate([left[t, :bs], left[t, bs:]], axis=1)
            rhs = jnp.concatenate(
                [
                    jnp.concatenate([b_re, b_im], axis=1),
                    jnp.concatenate([-b_im, b_re], axis=1),
                ],
                axis=0,
            )
            product = jnp.dot(lhs, rhs, preferred_element_type=jnp.float32)
            so_far = jnp.where(get(codes(t), "opens") > 0, product, so_far + product)
            for part in range(2):
                result[t, part] = so_far[:, part * bs : (part + 1) * bs].astype(result.dtype)
        total[...] = so_far
        for t in ids:
            code = codes(t)

            @pl.when((t < count) & (get(code, "closes") > 0))
            def _():
                store(result.at[t], out, get(code, "result"), store_sem).start()

        return carry

    lax.fori_loop(0, (count + UNROLL - 1) // UNROLL, some_terms, 0)

    def drain(t, carry):
        code = codes(t)

        @pl.when(get(code, "closes") > 0)
        def _():
            store(result.at[t], out, get(code, "result"), store_sem).wait()

        return carry

    lax.fori_loop(0, count, drain, 0)


def early_kernel(sizes, n_a, n_b, pieces_from, tables, c_cols, c_keep, *refs):
    rows, n_section, n_rows, panel_width, n_early, half = sizes
    strips, refs = refs[:n_section], refs[n_section:]
    a_bufs, b_bufs = refs[:n_a], refs[n_a : n_a + n_b]
    (
        out, late_codes, codes, empty, tails, table, numbers, scalars, zeros, sem, *scratch
    ) = refs[n_a + n_b :]
    left, right, _, _, load_sem, store_sem = scratch
    pieces_at = n_section
    wanted_at = pieces_at + n_rows
    lookup_at = wanted_at + rows
    results = c_cols.shape[1]
    me = lax.axis_index("rows") * n_section + lax.axis_index("section")
    copies = [pltpu.make_async_copy(tables.at[me], table, sem.at[0])]
    sources = [*strips, *(b_bufs[b] for b in pieces_from)]
    for n, source in enumerate(sources):
        tail = source.at[pl.ds(source.shape[0] - TAIL, TAIL)]
        copies.append(pltpu.make_async_copy(tail, tails.at[n], sem.at[1]))
    for copy in copies:
        copy.start()
    zeros[...] = jnp.zeros_like(zeros)
    numbers[wanted_at : wanted_at + rows, :results] = jnp.where(c_keep[...] > 0, c_cols[...], -2)
    for copy in copies:
        copy.wait()
    numbers[: len(sources)] = tails[...].astype(jnp.float32)[:, 0].astype(jnp.int32)
    numbers[lookup_at : lookup_at + 1] = table[:1]
    to_scalars = pltpu.make_async_copy(numbers, scalars, sem.at[0])
    to_scalars.start()
    to_scalars.wait()

    def lookup(n):
        return scalars[lookup_at, n]

    reciprocal = -(-(1 << 16) // rows)
    ks = np.arange(n_rows * rows)
    assert (ks * reciprocal >> 16 == ks // rows).all()
    low_bufs, high_bufs, cuts, strip_of = (
        [lookup(f * n_section + a) for a in range(n_section)] for f in range(4)
    )

    def one_row(i, counts):
        in_upper = i >= half
        columns, lates, parts = [], [], []
        for a in range(n_section):
            col = scalars[strip_of[a], i]
            k = jnp.maximum(a * panel_width + col, 0)
            group = (k * reciprocal) >> 16
            inside = k - group * rows
            piece = lookup(4 * n_section + 3 * n_rows + group)
            columns.append(jnp.where(col >= 0, scalars[pieces_at + piece, inside], -1))
            upper = inside >= rows // 2
            source = lookup(4 * n_section + jnp.where(upper, n_rows, 0) + group)
            inside = inside - jnp.where(upper, lookup(4 * n_section + 2 * n_rows + group), 0)
            buf = jnp.where(in_upper, high_bufs[a], low_bufs[a])
            lates.append((buf >= n_early).astype(jnp.int32))
            row = i - jnp.where(in_upper, cuts[a], 0)
            parts.append(put(left_buf=buf, left_row=row, right_buf=source, right_row=inside))
        n_now, n_late = counts
        for c in range(results):
            r = i * results + c
            wanted = scalars[wanted_at + i, c]
            matches = [(column == wanted).astype(jnp.int32) for column in columns]
            n_matches = sum(matches)
            late = functools.reduce(jnp.maximum, [m * l for m, l in zip(matches, lates)])
            empty[r] = n_matches

            @pl.when(n_matches == 0)
            def _():
                store(zeros, out, r, store_sem).start()

            @pl.when(n_matches > 0)
            def _():
                seen = jnp.int32(0)
                for m, part in zip(matches, parts):
                    @pl.when(m > 0)
                    def _():
                        opens = (seen == 0).astype(jnp.int32)
                        closes = (seen == n_matches - 1).astype(jnp.int32)
                        code = part + put(result=r, opens=opens, closes=closes)

                        @pl.when(late > 0)
                        def _():
                            late_codes[1 + n_late + seen] = code

                        @pl.when(late == 0)
                        def _():
                            codes[n_now + seen] = code
                            fetch(n_now + seen, code, a_bufs, b_bufs, left, right, load_sem)

                    seen = seen + m

            n_late = n_late + n_matches * late
            n_now = n_now + n_matches * (1 - late)
        return n_now, n_late

    n_now, n_late = lax.fori_loop(0, rows, one_row, (jnp.int32(0), jnp.int32(0)))
    late_codes[0] = n_late
    multiply(n_now, lambda t: codes[t], out, *scratch)

    def drain(r, carry):
        @pl.when(empty[r] == 0)
        def _():
            store(zeros, out, r, store_sem).wait()

        return carry

    lax.fori_loop(0, rows * results, drain, 0)


def late_kernel(n_a, n_b, codes, *refs):
    a_bufs, b_bufs = refs[:n_a], refs[n_a : n_a + n_b]
    out, *scratch = refs[n_a + n_b + 1 :]
    left, right, _, _, load_sem, _ = scratch

    def one(t, carry):
        fetch(t, codes[1 + t], a_bufs, b_bufs, left, right, load_sem)
        return carry

    lax.fori_loop(0, codes[0], one, 0)
    multiply(codes[0], lambda t: codes[1 + t], out, *scratch)


def scratch_for(most, bs):
    return [
        pltpu.VMEM((most, 2 * bs, bs), jnp.bfloat16),
        pltpu.VMEM((most, 2 * bs, bs), jnp.bfloat16),
        pltpu.VMEM((bs, 2 * bs), jnp.float32),
        pltpu.VMEM((most, 2, bs, bs), jnp.bfloat16),
        pltpu.SemaphoreType.DMA((most // UNROLL,)),
        pltpu.SemaphoreType.DMA,
    ]


def multiply_early(sizes, pieces_from, tables, c_cols, c_keep, strips, a_bufs, b_bufs, out_shape):
    rows, n_section, n_rows = sizes[:3]
    operands = [*strips, *a_bufs, *b_bufs]
    bs, n_results = out_shape[-1], c_cols.size
    most = rows * n_section + -(rows * n_section) % UNROLL
    n_tails = n_section + n_rows
    n_numbers = n_tails + rows + 1
    return pl.pallas_call(
        functools.partial(early_kernel, sizes, len(a_bufs), len(b_bufs), pieces_from),
        out_shape=(
            jax.ShapeDtypeStruct(out_shape, jnp.bfloat16),
            jax.ShapeDtypeStruct((1 + most,), jnp.int32),
        ),
        in_specs=[HBM, VMEM, VMEM] + [HBM] * len(operands),
        out_specs=(HBM, SMEM),
        scratch_shapes=[
            pltpu.SMEM((most,), jnp.int32),
            pltpu.SMEM((n_results,), jnp.int32),
            pltpu.VMEM((n_tails, TAIL, bs), jnp.bfloat16),
            pltpu.VMEM(tables.shape[1:], jnp.int32),
            pltpu.VMEM((n_numbers, bs), jnp.int32),
            pltpu.SMEM((n_numbers, bs), jnp.int32),
            pltpu.VMEM((2, bs, bs), jnp.bfloat16),
            pltpu.SemaphoreType.DMA((2,)),
            *scratch_for(most, bs),
        ],
        compiler_params=pltpu.CompilerParams(vmem_limit_bytes=VMEM_BYTES),
        cost_estimate=pl.CostEstimate(flops=1000, bytes_accessed=1000, transcendentals=0),
    )(tables, c_cols, c_keep, *operands)


def multiply_late(codes, a_bufs, b_bufs, so_far):
    operands = [codes, *a_bufs, *b_bufs, so_far]
    return pl.pallas_call(
        functools.partial(late_kernel, len(a_bufs), len(b_bufs)),
        out_shape=jax.ShapeDtypeStruct(so_far.shape, so_far.dtype),
        in_specs=[SMEM] + [HBM] * (len(operands) - 1),
        out_specs=HBM,
        scratch_shapes=scratch_for(codes.shape[0] - 1, so_far.shape[-1]),
        input_output_aliases={len(operands) - 1: 0},
        compiler_params=pltpu.CompilerParams(vmem_limit_bytes=VMEM_BYTES),
    )(*operands)


def on_device(x_blocks, x_cols, c_cols, c_keep):
    n_rows = lax.axis_size("rows")
    n_section = lax.axis_size("section")
    rows, bs = x_blocks.shape[0], x_blocks.shape[-1]
    panel_width = rows * n_rows // n_section
    half = rows // 2
    blocks, columns = x_blocks.reshape(-1, bs), x_cols.reshape(-1)
    everyone = [(r, s) for r in range(n_rows) for s in range(n_section)]
    tail = jnp.pad(columns.astype(blocks.dtype)[None], ((0, TAIL - 1), (0, bs - rows)))
    mine = jnp.concatenate([blocks, tail])

    if (n_rows, n_section) == (8, 4):
        swap = lambda x, m: lax.ppermute(x, "rows", [(r, r ^ m) for r in range(n_rows)])

        pairs = [(RING[i], RING[(i + 1) % 4]) for i in range(4)]
        step = lambda x: lax.ppermute(x, "section", pairs)
        half = 4
        middle = half * 2 * bs
        small, big = [jnp.concatenate([blocks[:middle], tail])], [blocks[middle:]]
        small.append(step(small[0]))
        big.append(step(big[0]))

        for_d, small[1] = lax.optimization_barrier((mine, small[1]))
        came = [swap(mine, 2), swap(mine, 4), swap(for_d, 6)]
        beside = swap(mine, 1)
        small.append(step(small[1]))
        big.append(step(big[1]))
        small.append(step(small[2]))
        past = [swap(came[0], 1), swap(came[1], 1)]
        big[2], beside = lax.optimization_barrier((big[2], beside))
        big.append(step(big[2]))

        cut = rows // 2 * 2 * bs
        lower, upper = came[2][:cut], came[2][cut:]
        lower, small[3] = lax.optimization_barrier((lower, small[3]))
        b_bufs = [mine, beside, *came, *past, swap(lower, 1), swap(upper, 1)]
        a_bufs = [mine, *small[1:], *big[1:]]
        n_early = 6
        strips = [mine, *small[1:]]

        pieces_from = (0, 1, 2, 5, 3, 6, 4, 8)
        steps = lambda s, a: (RING.index(s) - RING.index(a)) % 4
        tables = [
            [steps(s, a) for a in range(4)]
            + [(0, 4, 5, 6)[steps(s, a)] for a in range(4)]
            + [(0, half, half, half)[steps(s, a)] for a in range(4)]
            + [steps(s, a) for a in range(4)]
            + [(0, 1, 2, 5, 3, 6, 4, 7)[g ^ r] for g in range(8)]
            + [(0, 1, 2, 5, 3, 6, 4, 8)[g ^ r] for g in range(8)]
            + [(0, 0, 0, 0, 0, 0, 0, rows // 2)[g ^ r] for g in range(8)]
            + [g ^ r for g in range(8)]
            for r, s in everyone
        ]
    else:

        def shifts(x, axis, n):
            shift = lambda d: lax.ppermute(x, axis, [(p, (p + d) % n) for p in range(n)])
            return [x] + [shift(d) for d in range(1, n)]

        a_bufs, b_bufs = shifts(mine, "section", n_section), shifts(mine, "rows", n_rows)
        n_early, strips = n_section, a_bufs
        pieces_from = tuple(range(n_rows))
        tables = []
        for r, s in everyone:
            panels = [(s - a) % n_section for a in range(n_section)]
            groups = [(r - g) % n_rows for g in range(n_rows)]
            tables.append(panels * 2 + [0] * n_section + panels + groups * 2 + [0] * n_rows + groups)

    tables = np.array(tables, np.int32)
    assert tables.shape[1] <= bs
    tables = np.pad(tables, ((0, 0), (0, 8 * bs - tables.shape[1]))).reshape(len(everyone), 8, bs)
    sizes = (rows, n_section, n_rows, panel_width, n_early, half)
    out_shape = (rows, c_cols.shape[1], *x_blocks.shape[2:])
    out, codes = multiply_early(
        sizes, pieces_from, jnp.asarray(tables), c_cols, c_keep, strips, a_bufs[:n_early], b_bufs, out_shape
    )
    if n_early < len(a_bufs):
        out = multiply_late(codes, a_bufs, b_bufs, out)
    return out


def solution(mesh):
    in_specs = (
        P("rows", "section", None, None, None),
        P("rows", "section"),
        P("rows", "section"),
        P("rows", "section"),
    )
    out_specs = P("rows", "section", None, None, None)
    return jax.shard_map(
        on_device, mesh=mesh, in_specs=in_specs, out_specs=out_specs, check_vma=False
    )
```
